256 devices in a mesh: ha: 16 (over y, z_lo), wa: 8 (over x, z_hi), ta: 2 (over core).
Axes of the slice: x: 4, y: 4, z: 8 (z_hi: 2, z_lo: 4; z = z_hi * 4 + z_lo), core: 2. Of those that a mesh axis runs over, the one named last changes fastest.
Arguments:
- queries: bfloat16 [32, 16, 64, 1536], P('ha', None, 'wa', 'ta'), may hold values from -16 to 16
- key_video: bfloat16 [32, 16, 64, 1536], P('ha', None, 'wa', 'ta'), may hold values from -16 to 16
- value_video: bfloat16 [32, 16, 64, 1536], P('ha', None, 'wa', 'ta'), may hold values from -6 to 6
- grad_output: bfloat16 [32, 16, 64, 1536], P('ha', None, 'wa', 'ta'), may hold values from -6 to 6
- text_keys: bfloat16 [256, 1536], P(None, 'ta'), may hold values from -6 to 6
- text_values: bfloat16 [256, 1536], P(None, 'ta'), may hold values from -6 to 6
- window_reach: int32 [12, 6], P('ta'), may hold values from 0 to 1, as said below
- text_valid: int32 [256], replicated, may hold values from 0 to 1, as said below
Outputs:
- query_grad: bfloat16 [32, 16, 64, 1536], P('ha', None, 'wa', 'ta')
- key_grad: bfloat16 [32, 16, 64, 1536], P('ha', None, 'wa', 'ta')
- value_grad: bfloat16 [32, 16, 64, 1536], P('ha', None, 'wa', 'ta')
- text_key_grad: bfloat16 [256, 1536], P(None, 'ta')
- text_value_grad: bfloat16 [256, 1536], P(None, 'ta')
The draws below stay inside these ranges and needn't reach their ends.
Inputs may be any that keep to these rules, and one draw needn't show every extreme that they name: `window_reach`: heads 0 and 11 reach one tile in all six directions. `text_valid`: the first 64 entries are 1 and the last 64 entries are 0.
All inputs are finite; a program needn't handle non-finite values.
Results may differ from the reference program's by a relative error of at most 0.023.
Values may be sent and summed in bfloat16 or wider, within the bound.
No kernel may reach another device: no remote copies, remote signals or barrier semaphores. Data moves between devices by JAX's collectives and lax.ppermute only.
A program may use at most 192 MiB of HBM per device.

```python
import jax
import jax.numpy as jnp
from jax import lax

HEADS = 12
HD = 128
TILE = 8
TILE_T = 2
TEXT = 256
FR = 32
NH = 16
NW = 64


def draw_queries(key, part):
    key = jax.random.fold_in(key, 11)
    values = jax.random.truncated_normal(key, -4.0, 4.0, (FR, NH, NW, HEADS * HD), jnp.float32)
    return values.astype(jnp.bfloat16)


def draw_key_video(key, part):
    key = jax.random.fold_in(key, 12)
    first_key = jax.random.fold_in(key, 0)
    values = jax.random.truncated_normal(first_key, -4.0, 4.0, (FR, NH, NW, HEADS * HD), jnp.float32)
    return values.astype(jnp.bfloat16)


def draw_window_reach(key, part):
    key = jax.random.fold_in(key, 21)
    spans = jax.random.randint(key, (HEADS, 6), 0, 2, dtype=jnp.int32)
    head_ids = lax.broadcasted_iota(jnp.int32, (HEADS, 6), 0)
    pinned = (head_ids == 0) | (head_ids == HEADS - 1)
    return jnp.where(pinned, 1, spans).astype(jnp.int32)


def draw_text_valid(key, part):
    key = jax.random.fold_in(key, 31)
    middle = jax.random.randint(key, (TEXT,), 0, 2, dtype=jnp.int32)
    positions = lax.broadcasted_iota(jnp.int32, (TEXT,), 0)
    kept = jnp.where(positions < TEXT // 4, 1, middle)
    kept = jnp.where(positions >= TEXT - TEXT // 4, 0, kept)
    return kept.astype(jnp.int32)


def block_levels(stream_key, extent, shards, smallest, largest):
    level, own = 1.0, jax.random.fold_in(stream_key, 6)
    for axis_at, parts in shards:
        steps = jnp.exp(jax.random.uniform(jax.random.fold_in(own, axis_at), (parts,), jnp.float32, smallest / len(shards), largest / len(shards)))
        level = level * jnp.repeat(steps, extent[axis_at] // parts).reshape([-1 if axis == axis_at else 1 for axis in range(len(extent))])
    return level


def gaussian(stream_key, dims, scale, limit, cuts=(), held_as=jnp.bfloat16):
    values = jax.random.normal(stream_key, dims, jnp.float32) * scale
    if len(cuts) > 0:
        values = block_levels(stream_key, dims, cuts, -0.22, 0.18) * values
    return jnp.clip(values, min=-limit, max=limit).astype(held_as)


def setup_inputs(seed: int = 0) -> dict:
    arg_keys = jax.random.split(jax.random.key(seed), 9)
    queries = draw_queries(jax.random.fold_in(arg_keys[8], 71), 0)
    key_video = draw_key_video(jax.random.fold_in(arg_keys[8], 71), 0)
    value_video = gaussian(arg_keys[2], (FR, NH, NW, HEADS * HD), 1.0, 6.0, ((0, 16), (2, 8), (3, 2)))
    grad_output = gaussian(arg_keys[3], (FR, NH, NW, HEADS * HD), 1.0, 6.0, ((0, 16), (2, 8), (3, 2)))
    text_keys = gaussian(arg_keys[4], (TEXT, HEADS * HD), 1.0, 6.0, ((1, 2),))
    text_values = gaussian(arg_keys[5], (TEXT, HEADS * HD), 1.0, 6.0, ((1, 2),))
    window_reach = draw_window_reach(jax.random.fold_in(arg_keys[8], 71), 0)
    text_valid = draw_text_valid(jax.random.fold_in(arg_keys[8], 71), 0)
    return dict(queries=queries, key_video=key_video, value_video=value_video, grad_output=grad_output, text_keys=text_keys, text_values=text_values, window_reach=window_reach, text_valid=text_valid)


def to_tiles(grid):
    frame_count, height, width, feature_count = grid.shape
    split_grid = grid.reshape(frame_count // TILE_T, TILE_T, height // TILE, TILE, width // TILE, TILE, feature_count)
    moved = split_grid.transpose(0, 2, 4, 1, 3, 5, 6)
    return moved.reshape(frame_count // TILE_T, height // TILE, width // TILE, TILE_T * TILE * TILE, feature_count)


def from_tiles(tiled):
    time_tiles, row_tiles, col_tiles, tile_size, feature_count = tiled.shape
    split_tiles = tiled.reshape(time_tiles, row_tiles, col_tiles, TILE_T, TILE, TILE, feature_count)
    moved = split_tiles.transpose(0, 3, 1, 4, 2, 5, 6)
    return moved.reshape(time_tiles * TILE_T, row_tiles * TILE, col_tiles * TILE, feature_count)


def windows(padded, window_counts):
    time_tiles, row_tiles, col_tiles = window_counts
    pieces = [padded[time_step:time_step + time_tiles, row_step:row_step + row_tiles, col_step:col_step + col_tiles]
              for time_step in range(3) for row_step in range(3) for col_step in range(3)]
    stacked = jnp.stack(pieces, axis=3)
    return stacked.reshape((time_tiles * row_tiles * col_tiles, 27 * padded.shape[3]) + padded.shape[4:])


def window_mask(spans, firsts, window_counts, grid_counts, direction, tile_size):
    offsets = jnp.arange(3, dtype=jnp.int32) - 1
    valids = []
    for axis_index in range(3):
        near = firsts[axis_index] + jnp.arange(window_counts[axis_index], dtype=jnp.int32)[:, None] + offsets[None, :]
        reach = (direction * offsets >= -spans[2 * axis_index]) & (direction * offsets <= spans[2 * axis_index + 1])
        valids.append((near >= 0) & (near < grid_counts[axis_index]) & reach[None, :])
    joined = (valids[0][:, None, None, :, None, None] & valids[1][None, :, None, None, :, None]
              & valids[2][None, None, :, None, None, :])
    joined = jnp.broadcast_to(joined[..., None], tuple(window_counts) + (3, 3, 3, tile_size))
    return joined.reshape(window_counts[0] * window_counts[1] * window_counts[2], 27 * tile_size)


def output_delta_product(form, left, right):
    return jnp.einsum(form, left.astype(jnp.float32), right.astype(jnp.float32))


def query_side(query_piece, key_piece, value_piece, gradient_piece, text_key_piece, text_value_piece, key_mask, text_mask, logit_scale_factor):
    score_matrix = output_delta_product('vns,vys->vny', query_piece, key_piece) * logit_scale_factor
    text_scores = output_delta_product('bqe,te->bqt', query_piece, text_key_piece) * logit_scale_factor
    score_matrix = jnp.where(key_mask[:, None, :], score_matrix, -jnp.inf)
    text_scores = jnp.where(text_mask[None, None, :], text_scores, -jnp.inf)
    highest = jnp.maximum(jnp.max(score_matrix, axis=2), jnp.max(text_scores, axis=2))
    totals = jnp.sum(jnp.exp(score_matrix - highest[..., None]), axis=2) + jnp.sum(jnp.exp(text_scores - highest[..., None]), axis=2)
    log_totals = highest + jnp.log(totals)
    probs = jnp.exp(score_matrix - log_totals[..., None])
    text_probs = jnp.exp(text_scores - log_totals[..., None])
    probabilities_reduced = probs.astype(jnp.bfloat16)
    text_probabilities_reduced = text_probs.astype(jnp.bfloat16)
    attended_output = output_delta_product('djt,dth->djh', probabilities_reduced, value_piece) + output_delta_product('ikd,dx->ikx', text_probabilities_reduced, text_value_piece)
    deltas = jnp.sum(gradient_piece.astype(jnp.float32) * attended_output, axis=2)
    probability_gradients = output_delta_product('vns,vys->vny', gradient_piece, value_piece)
    text_prob_grads = output_delta_product('bqe,te->bqt', gradient_piece, text_value_piece)
    score_gradients = (probs * (probability_gradients - deltas[..., None]) * logit_scale_factor).astype(jnp.bfloat16)
    text_score_gradients = (text_probs * (text_prob_grads - deltas[..., None]) * logit_scale_factor).astype(jnp.bfloat16)
    query_gradients = output_delta_product('djt,dth->djh', score_gradients, key_piece) + output_delta_product('ikd,dx->ikx', text_score_gradients, text_key_piece)
    text_key_grads = output_delta_product('bqt,bqe->te', text_score_gradients, query_piece)
    text_value_grads = output_delta_product('bqt,bqe->te', text_probabilities_reduced, gradient_piece)
    return query_gradients, log_totals, deltas, text_key_grads, text_value_grads


def key_side(key_piece, value_piece, query_piece, gradient_piece, log_part, delta_part, query_mask, logit_scale_factor):
    score_matrix = output_delta_product('bke,bqe->bkq', key_piece, query_piece) * logit_scale_factor
    score_matrix = jnp.where(query_mask[:, None, :], score_matrix - log_part[:, None, :], -jnp.inf)
    probs = jnp.exp(score_matrix)
    probabilities_reduced = probs.astype(jnp.bfloat16)
    probability_gradients = output_delta_product('bke,bqe->bkq', value_piece, gradient_piece)
    score_gradients = (probs * (probability_gradients - delta_part[:, None, :]) * logit_scale_factor).astype(jnp.bfloat16)
    key_grads = output_delta_product('bkq,bqe->bke', score_gradients, query_piece)
    value_grads = output_delta_product('bkq,bqe->bke', probabilities_reduced, gradient_piece)
    return key_grads, value_grads


def reference(queries, key_video, value_video, grad_output, text_keys, text_values, window_reach, text_valid):
    time_tiles = queries.shape[0] // TILE_T
    row_tiles = queries.shape[1] // TILE
    col_tiles = queries.shape[2] // TILE
    tile_size = TILE_T * TILE * TILE
    batch_size = row_tiles * col_tiles
    grid_counts = (time_tiles, row_tiles, col_tiles)
    step_counts = (1, row_tiles, col_tiles)
    logit_scale_factor = HD ** -0.5
    text_mask = text_valid > 0
    border = ((1, 1), (1, 1), (1, 1), (0, 0), (0, 0))
    query_tile_rows = to_tiles(queries)
    gradient_tiles = to_tiles(grad_output)
    key_tiles = to_tiles(key_video)
    value_tiles = to_tiles(value_video)
    padded_keys = jnp.pad(key_tiles, border)
    padded_values = jnp.pad(value_tiles, border)

    def query_step(time_index):
        key_windows = windows(lax.dynamic_slice_in_dim(padded_keys, time_index, 3, 0), step_counts)
        value_windows = windows(lax.dynamic_slice_in_dim(padded_values, time_index, 3, 0), step_counts)
        step_queries = lax.dynamic_index_in_dim(query_tile_rows, time_index, 0, keepdims=False).reshape(batch_size, tile_size, -1)
        step_grads = lax.dynamic_index_in_dim(gradient_tiles, time_index, 0, keepdims=False).reshape(batch_size, tile_size, -1)
        query_parts, log_parts, delta_parts, text_key_parts, text_value_parts = [], [], [], [], []
        for head_index in range(HEADS):
            first_column, last_column = head_index * HD, (head_index + 1) * HD
            key_mask = window_mask(window_reach[head_index], (time_index, 0, 0), step_counts, grid_counts, 1, tile_size)
            query_gradients, log_totals, deltas, text_key_grads, text_value_grads = query_side(
                step_queries[:, :, first_column:last_column], key_windows[:, :, first_column:last_column], value_windows[:, :, first_column:last_column],
                step_grads[:, :, first_column:last_column], text_keys[:, first_column:last_column], text_values[:, first_column:last_column],
                key_mask, text_mask, logit_scale_factor)
            query_parts.append(query_gradients.astype(jnp.bfloat16))
            log_parts.append(log_totals[..., None])
            delta_parts.append(deltas[..., None])
            text_key_parts.append(text_key_grads)
            text_value_parts.append(text_value_grads)
        return (jnp.concatenate(query_parts, axis=2).reshape(row_tiles, col_tiles, tile_size, -1),
                jnp.concatenate(log_parts, axis=2).reshape(row_tiles, col_tiles, tile_size, HEADS),
                jnp.concatenate(delta_parts, axis=2).reshape(row_tiles, col_tiles, tile_size, HEADS),
                jnp.concatenate(text_key_parts, axis=1), jnp.concatenate(text_value_parts, axis=1))

    query_grid, log_grid, delta_grid, text_key_rows, text_value_rows = lax.map(query_step, jnp.arange(time_tiles, dtype=jnp.int32))
    padded_queries = jnp.pad(query_tile_rows, border)
    padded_grads = jnp.pad(gradient_tiles, border)
    padded_logs = jnp.pad(log_grid, border)
    padded_deltas = jnp.pad(delta_grid, border)

    def key_step(time_index):
        query_windows = windows(lax.dynamic_slice_in_dim(padded_queries, time_index, 3, 0), step_counts)
        grad_windows = windows(lax.dynamic_slice_in_dim(padded_grads, time_index, 3, 0), step_counts)
        log_windows = windows(lax.dynamic_slice_in_dim(padded_logs, time_index, 3, 0), step_counts)
        delta_windows = windows(lax.dynamic_slice_in_dim(padded_deltas, time_index, 3, 0), step_counts)
        step_keys = lax.dynamic_index_in_dim(key_tiles, time_index, 0, keepdims=False).reshape(batch_size, tile_size, -1)
        step_values = lax.dynamic_index_in_dim(value_tiles, time_index, 0, keepdims=False).reshape(batch_size, tile_size, -1)
        key_parts, value_parts = [], []
        for head_index in range(HEADS):
            first_column, last_column = head_index * HD, (head_index + 1) * HD
            query_mask = window_mask(window_reach[head_index], (time_index, 0, 0), step_counts, grid_counts, -1, tile_size)
            key_grads, value_grads = key_side(
                step_keys[:, :, first_column:last_column], step_values[:, :, first_column:last_column],
                query_windows[:, :, first_column:last_column], grad_windows[:, :, first_column:last_column],
                log_windows[:, :, head_index], delta_windows[:, :, head_index], query_mask, logit_scale_factor)
            key_parts.append(key_grads.astype(jnp.bfloat16))
            value_parts.append(value_grads.astype(jnp.bfloat16))
        return (jnp.concatenate(key_parts, axis=2).reshape(row_tiles, col_tiles, tile_size, -1),
                jnp.concatenate(value_parts, axis=2).reshape(row_tiles, col_tiles, tile_size, -1))

    key_grid, value_grid = lax.map(key_step, jnp.arange(time_tiles, dtype=jnp.int32))
    query_grad = from_tiles(query_grid)
    key_grad = from_tiles(key_grid)
    value_grad = from_tiles(value_grid)
    text_key_grad = jnp.sum(text_key_rows, axis=0).astype(jnp.bfloat16)
    text_value_grad = jnp.sum(text_value_rows, axis=0).astype(jnp.bfloat16)
    return query_grad, key_grad, value_grad, text_key_grad, text_value_grad
```

```python
import functools

import jax
import jax.numpy as jnp
import numpy as np
from jax import lax
from jax.experimental import pallas as pl
from jax.experimental.pallas import tpu as pltpu
from jax.sharding import PartitionSpec as P

HD = 128
TILE = 8
TILE_T = 2
AXES = ("ha", "wa")
FRAME_PARTS = 16
COL_PARTS = 8
RUN = 4
HEADS = 3
HALF = HEADS * HD
PAIR = 2 * HD
BLOCK = 256
SCALE = HD**-0.5
EXP_SCALE = SCALE * float(np.log2(np.e))
COLS = ((0, 256), (0, 512), (0, 512), (256, 512))


def move(block, step):
    route = []
    for ha in range(FRAME_PARTS):
        for wa in range(COL_PARTS):
            there_ha, there_wa = step(ha, wa)
            if 0 <= there_ha < FRAME_PARTS and 0 <= there_wa < COL_PARTS:
                route.append((ha * COL_PARTS + wa, there_ha * COL_PARTS + there_wa))
    return lax.ppermute(block, AXES, route)


def across(ha, wa):
    return ha, wa ^ 1


def frames_by(distance):
    def step(ha, wa):
        there = ha + distance
        return there, wa ^ ((ha // RUN ^ there // RUN) & 1)

    return step


def cols_by(distance):
    return lambda ha, wa: (ha, wa + 2 * distance)


def flip(ha_bits, wa_bits):
    return lambda ha, wa: (ha ^ ha_bits, wa ^ wa_bits)


def lanes(start, count=HD):
    return pl.ds(pl.multiple_of(start, HD), count)


def split_kernel(group_ref, first_ref, second_ref, send_ref, keep_ref):
    group = group_ref[0]
    for out_ref, start in ((send_ref, (1 - group) * HALF), (keep_ref, group * HALF)):
        for head in range(HEADS):
            at = head * PAIR
            out_ref[:, at : at + HD] = first_ref[0, 0, :, lanes(start + head * HD)]
            out_ref[:, at + HD : at + PAIR] = second_ref[0, 0, :, lanes(start + head * HD)]


def split_heads(group, first, second):
    shape = (TILE_T, 2, TILE * TILE, 2 * HALF)
    rows = TILE * TILE
    source = pl.BlockSpec((1, 1, rows, 2 * HALF), lambda i, g: (i % 2, i // 2, 0, 0))
    target = pl.BlockSpec((rows, 2 * HALF), lambda i, g: (i, 0))
    out = jax.ShapeDtypeStruct((BLOCK, 2 * HALF), jnp.bfloat16)
    return pl.pallas_call(
        split_kernel,
        out_shape=(out, out),
        grid_spec=pltpu.PrefetchScalarGridSpec(
            num_scalar_prefetch=1, grid=(4,), in_specs=[source, source], out_specs=(target, target)
        ),
        cost_estimate=pl.CostEstimate(flops=0, bytes_accessed=1600000, transcendentals=0),
        name="split_heads",
    )(group, first.reshape(shape), second.reshape(shape))


def join_pair_kernel(group_ref, keep_ref, got_ref, first_ref, second_ref):
    group = group_ref[0]
    for in_ref, start in ((keep_ref, group * HALF), (got_ref, (1 - group) * HALF)):
        for head in range(HEADS):
            at = head * PAIR
            first_ref[0, 0, :, lanes(start + head * HD)] = in_ref[:, at : at + HD]
            second_ref[0, 0, :, lanes(start + head * HD)] = in_ref[:, at + HD : at + PAIR]


def join_one_kernel(group_ref, keep_ref, got_ref, out_ref):
    group = group_ref[0]
    for in_ref, start in ((keep_ref, group * HALF), (got_ref, (1 - group) * HALF)):
        out_ref[0, 0, :, lanes(start, HALF)] = in_ref[...]


def join_heads(group, keep, got, kernel, count):
    rows = TILE * TILE
    source = pl.BlockSpec((rows, keep.shape[1]), lambda i, g: (i, 0))
    target = pl.BlockSpec((1, 1, rows, 2 * HALF), lambda i, g: (i % 2, i // 2, 0, 0))
    out = jax.ShapeDtypeStruct((TILE_T, 2, rows, 2 * HALF), jnp.bfloat16)
    parts = pl.pallas_call(
        kernel,
        out_shape=(out,) * count,
        grid_spec=pltpu.PrefetchScalarGridSpec(
            num_scalar_prefetch=1,
            grid=(4,),
            in_specs=[source, source],
            out_specs=(target,) * count,
        ),
        cost_estimate=pl.CostEstimate(flops=0, bytes_accessed=800000 * count, transcendentals=0),
        name="join_heads",
    )(group, keep, got)
    return [part.reshape(TILE_T, 2 * TILE, TILE, 2 * HALF) for part in parts]


def dot_t(left, right):
    return lax.dot_general(
        left, right, (((1,), (1,)), ((), ())), preferred_element_type=jnp.float32
    )


def dot(left, right):
    return lax.dot_general(
        left, right, (((1,), (0,)), ((), ())), preferred_element_type=jnp.float32
    )


def t_dot(left, right):
    return lax.dot_general(
        left, right, (((0,), (0,)), ((), ())), preferred_element_type=jnp.float32
    )


def fold(values, op):
    return op(values.reshape(values.shape[0] // 8, 8, values.shape[1]), axis=0)


def attend_kernel(flag_ref, bias_ref, text_bias_ref, qg_ref, text_ref, *refs):
    kv_refs, (grad_refs, dq_ref, dtext_ref) = refs[:12], (refs[12:24], refs[24], refs[25])
    p_ref, dp_ref, high_ref, total_ref, delta_ref, dq_sum_ref = refs[26:]
    head = pl.program_id(0)

    def visible(block):
        return flag_ref[head * 12 + block] != 0

    def q(low, high):
        return qg_ref[low:high, :HD]

    def g(low, high):
        return qg_ref[low:high, HD:]

    def rows(block):
        return slice(block * BLOCK, (block + 1) * BLOCK)

    scores = dot_t(text_ref[:, :HD], q(0, 512)) + text_bias_ref[:, :1]
    p_ref[rows(12), :] = scores
    high_ref[...] = fold(scores, jnp.max)
    for block in range(12):
        low, high = COLS[block % 4]

        @pl.when(visible(block))
        def _(block=block, low=low, high=high):
            scores = dot_t(kv_refs[block][:, :HD], q(low, high))
            for half in range(2):
                part = scores[half * 128 : half * 128 + 128]
                part = part + bias_ref[0, 2 * block + half, low:high][None, :]
                at = block * BLOCK + half * 128
                p_ref[at : at + 128, low:high] = part
                high_ref[:, low:high] = jnp.maximum(high_ref[:, low:high], fold(part, jnp.max))

    highest = jnp.max(high_ref[...], axis=0, keepdims=True)
    total_ref[...] = jnp.zeros_like(total_ref)
    delta_ref[...] = jnp.zeros_like(delta_ref)

    def weigh(block, value, low, high):
        p = jnp.exp2((p_ref[rows(block), low:high] - highest[:, low:high]) * EXP_SCALE)
        dp = dot_t(value, g(low, high))
        p_ref[rows(block), low:high] = p
        dp_ref[rows(block), low:high] = dp
        total_ref[:, low:high] += fold(p, jnp.sum)
        delta_ref[:, low:high] += fold(p * dp, jnp.sum)

    weigh(12, text_ref[:, HD:], 0, 512)
    for block in range(12):
        low, high = COLS[block % 4]

        @pl.when(visible(block))
        def _(block=block, low=low, high=high):
            weigh(block, kv_refs[block][:, HD:], low, high)

    inverse = 1.0 / jnp.sum(total_ref[...], axis=0, keepdims=True)
    delta = jnp.sum(delta_ref[...], axis=0, keepdims=True) * inverse
    scaled = inverse * SCALE

    def spread(block, key, out_ref, low, high):
        p = p_ref[rows(block), low:high]
        prob = (p * inverse[:, low:high]).astype(jnp.bfloat16)
        ds = p * scaled[:, low:high] * (dp_ref[rows(block), low:high] - delta[:, low:high])
        ds = ds.astype(jnp.bfloat16)
        out_ref[:, :HD] = dot(ds, q(low, high)).astype(jnp.bfloat16)
        out_ref[:, HD:] = dot(prob, g(low, high)).astype(jnp.bfloat16)
        return t_dot(ds, key)

    dq_sum_ref[...] = spread(12, text_ref[:, :HD], dtext_ref, 0, 512)
    for block in range(12):
        low, high = COLS[block % 4]

        @pl.when(visible(block))
        def _(block=block, low=low, high=high):
            dq_sum_ref[low:high, :] += spread(
                block, kv_refs[block][:, :HD], grad_refs[block], low, high
            )

        @pl.when(jnp.logical_not(visible(block)))
        def _(block=block):
            grad_refs[block][...] = jnp.zeros_like(grad_refs[block])

    dq_ref[...] = dq_sum_ref[...].astype(jnp.bfloat16)


def attend(flags, bias, text_bias, qg, text, blocks):
    pair = pl.BlockSpec((BLOCK, PAIR), lambda h, f: (0, h))
    out = jax.ShapeDtypeStruct((BLOCK, 2 * HALF), jnp.bfloat16)
    results = pl.pallas_call(
        attend_kernel,
        out_shape=(out,) * 12 + (jax.ShapeDtypeStruct((2 * BLOCK, HALF), jnp.bfloat16), out),
        grid_spec=pltpu.PrefetchScalarGridSpec(
            num_scalar_prefetch=1,
            grid=(HEADS,),
            in_specs=[
                pl.BlockSpec((1, 24, 2 * BLOCK), lambda h, f: (h, 0, 0)),
                pl.BlockSpec((BLOCK, HD), lambda h, f: (0, 0)),
                pl.BlockSpec((2 * BLOCK, PAIR), lambda h, f: (0, h)),
                pair,
            ]
            + [pair] * 12,
            out_specs=(pair,) * 12 + (pl.BlockSpec((2 * BLOCK, HD), lambda h, f: (0, h)), pair),
            scratch_shapes=[
                pltpu.VMEM((13 * BLOCK, 2 * BLOCK), jnp.float32),
                pltpu.VMEM((13 * BLOCK, 2 * BLOCK), jnp.float32),
                pltpu.VMEM((8, 2 * BLOCK), jnp.float32),
                pltpu.VMEM((8, 2 * BLOCK), jnp.float32),
                pltpu.VMEM((8, 2 * BLOCK), jnp.float32),
                pltpu.VMEM((2 * BLOCK, HD), jnp.float32),
            ],
        ),
        compiler_params=pltpu.CompilerParams(vmem_limit_bytes=40 * 1024 * 1024),
        cost_estimate=pl.CostEstimate(
            flops=10 * 512 * 2560 * HD * HEADS,
            bytes_accessed=12000000,
            transcendentals=512 * 2560 * HEADS,
        ),
        name="attend",
    )(flags, bias, text_bias, qg, text, *blocks)
    return results[:12], results[12], results[13]


def visibility(reach, ha, wa):
    between = lambda d, low, high: (d >= -low) & (d <= high)
    column = wa // 2 * 2
    s = jnp.arange(3, dtype=jnp.int32) - 1
    frames = between(s[None, :], reach[:, 0:1], reach[:, 1:2])
    frames = frames & (ha + s >= 0)[None, :] & (ha + s < FRAME_PARTS)[None, :]
    two = jnp.arange(2, dtype=jnp.int32)
    r = two[:, None] - two[None, :]
    rows = between(r[None], reach[:, 2, None, None], reach[:, 3, None, None])
    c = jnp.arange(4, dtype=jnp.int32) - 1
    d = c[:, None] - two[None, :]
    cols = between(d[None], reach[:, 4, None, None], reach[:, 5, None, None])
    cols = cols & ((column + c >= 0) & (column + c < COL_PARTS))[None, :, None]
    seen = (
        frames[:, :, None, None, None, None]
        & cols[:, None, :, None, :, None]
        & rows[:, None, None, :, None, :]
    )
    flags = jnp.any(seen, axis=(3, 4, 5)).astype(jnp.int32).reshape(HEADS * 12)
    bias = jnp.where(seen, 0.0, -jnp.inf).astype(jnp.float32).reshape(HEADS, 24, 4, 1)
    bias = jnp.broadcast_to(bias, (HEADS, 24, 4, 128)).reshape(HEADS, 24, 512)
    return flags, bias


def added(*parts):
    total = parts[0].astype(jnp.float32)
    for part in parts[1:]:
        total = total + part.astype(jnp.float32)
    return total.astype(jnp.bfloat16)


def sum_text(part, group, ha, wa):
    y, x = ha // RUN, wa // 2
    upper = y // 2
    other = lax.dynamic_slice_in_dim(part, (1 - upper) * 128, 128, 0)
    part = added(
        lax.dynamic_slice_in_dim(part, upper * 128, 128, 0), move(other, flip(2 * RUN, 0))
    )
    pieces = [
        move(lax.dynamic_slice_in_dim(part, (x ^ d) * 32, 32, 0), flip(0, 2 * d))
        for d in (1, 2, 3)
    ]
    part = added(lax.dynamic_slice_in_dim(part, x * 32, 32, 0), *pieces)
    near = [move(part, flip(d, 0)).astype(jnp.float32) for d in (1, 2, 3)]
    part = ((part.astype(jnp.float32) + near[0]) + (near[1] + near[2])).astype(jnp.bfloat16)
    mine = added(part, move(part, flip(RUN, 1)))
    theirs = added(move(part, flip(RUN, 0)), move(part, flip(0, 1)))
    both = jnp.stack(
        [jnp.where(group == 0, mine, theirs), jnp.where(group == 0, theirs, mine)], axis=0
    )
    quarter = jnp.zeros((4,) + both.shape, both.dtype)
    quarter = lax.dynamic_update_index_in_dim(quarter, both, x, 0)
    for d in (1, 2, 3):
        quarter = lax.dynamic_update_index_in_dim(quarter, move(both, flip(0, 2 * d)), x ^ d, 0)
    distant = move(quarter, flip(2 * RUN, 0))
    whole = jnp.stack(
        [jnp.where(upper == 0, quarter, distant), jnp.where(upper == 0, distant, quarter)], axis=0
    )
    whole = whole.reshape(2, 4, 2, 32, HEADS, 2, HD)
    whole = whole.transpose(5, 0, 1, 3, 2, 4, 6).reshape(2, 256, 2 * HALF)
    return whole[0], whole[1]


def body(
    queries, key_video, value_video, grad_output, text_keys, text_values, window_reach, text_valid
):
    ha, wa = lax.axis_index("ha"), lax.axis_index("wa")
    side = wa % 2
    group = (side + ha // RUN) % 2
    group_at = group.reshape(1).astype(jnp.int32)

    def placed(keep, got):
        return jnp.where(side == 0, keep, got), jnp.where(side == 0, got, keep)

    send_kv, keep_kv = split_heads(group_at, key_video, value_video)
    own = placed(keep_kv, move(send_kv, across))
    send_qg, keep_qg = split_heads(group_at, queries, grad_output)
    earlier = [move(block, frames_by(1)) for block in own]
    later = [move(block, frames_by(-1)) for block in own]
    send_qg, earlier, later = lax.optimization_barrier((send_qg, earlier, later))
    qg = jnp.concatenate(placed(keep_qg, move(send_qg, across)), axis=0)

    blocks = []
    for left, right in (earlier, own, later):
        blocks += [move(right, cols_by(1)), left, right, move(left, cols_by(-1))]

    reach = lax.dynamic_slice_in_dim(window_reach, group * HEADS, HEADS, 0)
    flags, bias = visibility(reach, ha, wa)
    text_bias = jnp.where(text_valid > 0, 0.0, -jnp.inf).astype(jnp.float32)
    text_bias = jnp.broadcast_to(text_bias[:, None], (256, HD))
    text = jnp.stack(
        [
            lax.dynamic_slice_in_dim(t, group * HALF, HALF, 1).reshape(256, HEADS, HD)
            for t in (text_keys, text_values)
        ],
        axis=2,
    ).reshape(256, 2 * HALF)

    grads, dq, dtext = attend(flags, bias, text_bias, qg, text, blocks)

    def columns_in(step):
        beyond_left, left, right, beyond_right = grads[4 * step : 4 * step + 4]
        return (left, move(beyond_right, cols_by(1))), (right, move(beyond_left, cols_by(-1)))

    outer = []
    for step, distance in ((0, -1), (2, 1)):
        outer.append([move(added(*parts), frames_by(distance)) for parts in columns_in(step)])
    totals = [
        added(*parts, first, second) for parts, first, second in zip(columns_in(1), *outer)
    ]

    text_key_grad, text_value_grad = sum_text(dtext, group, ha, wa)

    dq_own = jnp.where(side == 0, dq[:BLOCK], dq[BLOCK:])
    dq_other = jnp.where(side == 0, dq[BLOCK:], dq[:BLOCK])
    (query_grad,) = join_heads(group_at, dq_own, move(dq_other, across), join_one_kernel, 1)
    keep = jnp.where(side == 0, totals[0], totals[1])
    send = jnp.where(side == 0, totals[1], totals[0])
    key_grad, value_grad = join_heads(group_at, keep, move(send, across), join_pair_kernel, 2)
    return query_grad, key_grad, value_grad, text_key_grad, text_value_grad


def solution(mesh):
    video = P("ha", None, "wa", "ta")
    text = P(None, "ta")
    return jax.shard_map(
        body,
        mesh=mesh,
        in_specs=(video, video, video, video, text, text, P("ta", None), P()),
        out_specs=(video, video, video, text, text),
        check_vma=False,
    )
```

```python
import functools

import jax
import jax.numpy as jnp
import numpy as np
from jax import lax
from jax.experimental import pallas as pl
from jax.experimental.pallas import tpu as pltpu
from jax.sharding import PartitionSpec as P

HD = 128
TILE = 8
TILE_T = 2
AXES = ("ha", "wa")
FRAME_PARTS = 16
COL_PARTS = 8
RUN = 4
HEADS = 3
HALF = HEADS * HD
PAIR = 2 * HD
BLOCK = 256
TEXT = 192
SCALE = HD**-0.5
EXP_SCALE = SCALE * float(np.log2(np.e))
GROUPS = ((4,), (7,), (1, 2), (0,), (3,), (9, 10), (8,), (11,))
TILE_PARTS = ((0, 0, 0), (64, 1, 0), (128, 0, 1), (192, 1, 1))
COLS = ((0, 256), (0, 512), (0, 512), (256, 512))


def move(block, step):
    route = []
    for ha in range(FRAME_PARTS):
        for wa in range(COL_PARTS):
            there_ha, there_wa = step(ha, wa)
            if 0 <= there_ha < FRAME_PARTS and 0 <= there_wa < COL_PARTS:
                route.append((ha * COL_PARTS + wa, there_ha * COL_PARTS + there_wa))
    return lax.ppermute(block, AXES, route)


def across(ha, wa):
    return ha, wa ^ 1


def frames_by(distance):
    def step(ha, wa):
        there = ha + distance
        return there, wa ^ ((ha // RUN ^ there // RUN) & 1)

    return step


def cols_by(distance):
    return lambda ha, wa: (ha, wa + 2 * distance)


def flip(ha_bits, wa_bits):
    return lambda ha, wa: (ha ^ ha_bits, wa ^ wa_bits)


def lanes(start, count=HD):
    return pl.ds(pl.multiple_of(start, HD), count)


def split_kernel(group_ref, first_ref, second_ref, send_ref, keep_ref):
    group = group_ref[0]
    for out_ref, start in ((send_ref, (1 - group) * HALF), (keep_ref, group * HALF)):
        for at, frame, row in TILE_PARTS:
            for head in range(HEADS):
                for ref, low in ((first_ref, head * PAIR), (second_ref, head * PAIR + HD)):
                    part = ref[frame, row, :, lanes(start + head * HD)]
                    out_ref[at : at + 64, low : low + HD] = part


def split_heads(group, first, second):
    shape = (TILE_T, 2, TILE * TILE, 2 * HALF)
    source = pl.BlockSpec(shape, lambda i, g: (0, 0, 0, 0))
    target = pl.BlockSpec((BLOCK, 2 * HALF), lambda i, g: (0, 0))
    out = jax.ShapeDtypeStruct((BLOCK, 2 * HALF), jnp.bfloat16)
    return pl.pallas_call(
        split_kernel,
        out_shape=(out, out),
        grid_spec=pltpu.PrefetchScalarGridSpec(
            num_scalar_prefetch=1, grid=(1,), in_specs=[source, source], out_specs=(target, target)
        ),
        cost_estimate=pl.CostEstimate(flops=0, bytes_accessed=1600000, transcendentals=0),
        name="split_heads",
    )(group, first.reshape(shape), second.reshape(shape))


def join_pair_kernel(group_ref, keep_ref, got_ref, first_ref, second_ref):
    group = group_ref[0]
    for in_ref, start in ((keep_ref, group * HALF), (got_ref, (1 - group) * HALF)):
        for at, frame, row in TILE_PARTS:
            for head in range(HEADS):
                for ref, low in ((first_ref, head * PAIR), (second_ref, head * PAIR + HD)):
                    part = in_ref[at : at + 64, low : low + HD]
                    ref[frame, row, :, lanes(start + head * HD)] = part


def join_one_kernel(group_ref, keep_ref, got_ref, out_ref):
    group = group_ref[0]
    for in_ref, start in ((keep_ref, group * HALF), (got_ref, (1 - group) * HALF)):
        for at, frame, row in TILE_PARTS:
            out_ref[frame, row, :, lanes(start, HALF)] = in_ref[at : at + 64, :]


def join_heads(group, keep, got, kernel, count):
    shape = (TILE_T, 2, TILE * TILE, 2 * HALF)
    source = pl.BlockSpec(keep.shape, lambda i, g: (0, 0))
    target = pl.BlockSpec(shape, lambda i, g: (0, 0, 0, 0))
    out = jax.ShapeDtypeStruct(shape, jnp.bfloat16)
    parts = pl.pallas_call(
        kernel,
        out_shape=(out,) * count,
        grid_spec=pltpu.PrefetchScalarGridSpec(
            num_scalar_prefetch=1,
            grid=(1,),
            in_specs=[source, source],
            out_specs=(target,) * count,
        ),
        cost_estimate=pl.CostEstimate(flops=0, bytes_accessed=800000 * count, transcendentals=0),
        name="join_heads",
    )(group, keep, got)
    return [part.reshape(TILE_T, 2 * TILE, TILE, 2 * HALF) for part in parts]


def dot_t(left, right):
    return lax.dot_general(
        left, right, (((1,), (1,)), ((), ())), preferred_element_type=jnp.float32
    )


def dot(left, right):
    return lax.dot_general(
        left, right, (((1,), (0,)), ((), ())), preferred_element_type=jnp.float32
    )


def t_dot(left, right):
    return lax.dot_general(
        left, right, (((0,), (0,)), ((), ())), preferred_element_type=jnp.float32
    )


def fold(values, op):
    return op(values.reshape(values.shape[0] // 8, 8, values.shape[1]), axis=0)


def attend_kernel(flag_ref, bias_ref, text_bias_ref, qg_ref, text_ref, *refs):
    kv_refs, far_refs, mid_refs = refs[:12], refs[12:14], refs[14:17]
    dq_refs, dtext_ref, side_refs = refs[17:19], refs[19], refs[20:22]
    p_ref, dp_ref, high_ref, total_ref, delta_ref, dq_sum_ref = refs[22:]
    head = pl.program_id(0)

    def visible(block):
        return flag_ref[head * 12 + block] != 0

    def q(low, high):
        return qg_ref[low:high, :HD]

    def g(low, high):
        return qg_ref[low:high, HD:]

    def rows(block):
        return slice(block * BLOCK, block * BLOCK + (TEXT if block == 12 else BLOCK))

    def grad(block):
        step, column = divmod(block, 4)
        if column in (1, 2):
            return mid_refs[step].at[rows(column - 1), :]
        if step == 1:
            return side_refs[column // 3]
        return far_refs[column // 3].at[rows(step // 2), :]

    def spare(block):
        return slice(block * 8, block * 8 + 8)

    def weigh(block, pair_ref, bias, low, high, start=False):
        width = high - low
        scores = dot_t(pair_ref[:, :HD], q(low, high))
        dp = dot_t(pair_ref[:, HD:], g(low, high))
        dp_ref[rows(block), low:high] = dp
        if start:
            scores = scores + bias
        else:
            scores = (scores.reshape(2, 128, width) + bias[:, None, :]).reshape(BLOCK, width)
        highest = fold(scores, jnp.max)
        if not start:
            old = high_ref[spare(12), low:high]
            highest = jnp.maximum(old, highest)
            shrink = jnp.exp2((old - highest) * EXP_SCALE)
        p = jnp.exp2((scores.reshape(-1, 8, width) - highest[None]) * EXP_SCALE)
        total, delta = jnp.sum(p, axis=0), jnp.sum(p * dp.reshape(-1, 8, width), axis=0)
        p_ref[rows(block), low:high] = p.reshape(-1, width)
        if not start:
            total = total + total_ref[:, low:high] * shrink
            delta = delta + delta_ref[:, low:high] * shrink
            high_ref[spare(block), low:high] = highest
        else:
            high_ref[spare(13), low:high] = highest
        high_ref[spare(12), low:high] = highest
        total_ref[:, low:high] = total
        delta_ref[:, low:high] = delta

    weigh(12, text_ref, text_bias_ref[:, :1], 0, 512, start=True)
    def weigh_all(group):
        for block in group:
            low, high = COLS[block % 4]
            bias = bias_ref[0, 2 * block : 2 * block + 2, low:high]
            weigh(block, kv_refs[block], bias, low, high)

    weigh_all((5, 6))
    for group in GROUPS:
        pl.when(visible(group[0]))(functools.partial(weigh_all, group))

    last = high_ref[spare(12), :]
    highest = jnp.max(last, axis=0, keepdims=True)
    shrink = jnp.exp2((last - highest) * EXP_SCALE)
    inverse = 1.0 / jnp.sum(total_ref[...] * shrink, axis=0, keepdims=True)
    delta = jnp.sum(delta_ref[...] * shrink, axis=0, keepdims=True) * inverse

    def spread(block, key, out_ref, low, high):
        width = high - low
        at = spare(block + (block == 12))
        shrink = jnp.exp2((high_ref[at, low:high] - highest[:, low:high]) * EXP_SCALE)
        shrink = shrink * inverse[:, low:high]
        prob = p_ref[rows(block), low:high].reshape(-1, 8, width) * shrink[None]
        prob = prob.reshape(-1, width)
        ds = prob * ((dp_ref[rows(block), low:high] - delta[:, low:high]) * SCALE)
        ds = ds.astype(jnp.bfloat16)
        prob = prob.astype(jnp.bfloat16)
        out_ref[:, :HD] = dot(ds, q(low, high)).astype(jnp.bfloat16)
        out_ref[:, HD:] = dot(prob, g(low, high)).astype(jnp.bfloat16)
        return t_dot(key, ds)

    dq_sum_ref[...] = spread(12, text_ref[:, :HD], dtext_ref, 0, 512)
    def spread_all(group):
        for block in group:
            low, high = COLS[block % 4]
            dq_sum_ref[:, low:high] += spread(
                block, kv_refs[block][:, :HD], grad(block), low, high
            )

    def clear_all(group):
        for block in group:
            grad(block)[...] = jnp.zeros((BLOCK, PAIR), jnp.bfloat16)

    spread_all((5, 6))
    for group in GROUPS:
        pl.when(visible(group[0]))(functools.partial(spread_all, group))
        pl.when(jnp.logical_not(visible(group[0])))(functools.partial(clear_all, group))

    mirrored = flag_ref[36] != 0
    for ref, low, high in zip(dq_refs, (0, BLOCK), (BLOCK, 0)):
        sums = jnp.where(
            mirrored, dq_sum_ref[:, high : high + BLOCK], dq_sum_ref[:, low : low + BLOCK]
        )
        ref[...] = sums.T.astype(jnp.bfloat16)


def attend(flags, bias, text_bias, qg, text, blocks):
    pair = pl.BlockSpec((BLOCK, PAIR), lambda h, f: (0, h))
    text_pair = pl.BlockSpec((TEXT, PAIR), lambda h, f: (0, h))
    text_out = jax.ShapeDtypeStruct((TEXT, 2 * HALF), jnp.bfloat16)
    wide = pl.BlockSpec((2 * BLOCK, PAIR), lambda h, f: (0, h))
    out = jax.ShapeDtypeStruct((BLOCK, 2 * HALF), jnp.bfloat16)
    wide_out = jax.ShapeDtypeStruct((2 * BLOCK, 2 * HALF), jnp.bfloat16)
    results = pl.pallas_call(
        attend_kernel,
        out_shape=(wide_out,) * 2
        + (wide_out,) * 3
        + (jax.ShapeDtypeStruct((BLOCK, HALF), jnp.bfloat16),) * 2
        + (text_out,)
        + (out,) * 2,
        grid_spec=pltpu.PrefetchScalarGridSpec(
            num_scalar_prefetch=1,
            grid=(HEADS,),
            in_specs=[
                pl.BlockSpec((1, 24, 2 * BLOCK), lambda h, f: (h, 0, 0)),
                pl.BlockSpec((TEXT, HD), lambda h, f: (0, 0)),
                pl.BlockSpec((2 * BLOCK, PAIR), lambda h, f: (0, h)),
                text_pair,
            ]
            + [pair] * 12,
            out_specs=(wide,) * 2
            + (wide,) * 3
            + (pl.BlockSpec((BLOCK, HD), lambda h, f: (0, h)),) * 2
            + (text_pair,)
            + (pair,) * 2,
            scratch_shapes=[
                pltpu.VMEM((13 * BLOCK, 2 * BLOCK), jnp.float32),
                pltpu.VMEM((13 * BLOCK, 2 * BLOCK), jnp.float32),
                pltpu.VMEM((8 * 14, 2 * BLOCK), jnp.float32),
                pltpu.VMEM((8, 2 * BLOCK), jnp.float32),
                pltpu.VMEM((8, 2 * BLOCK), jnp.float32),
                pltpu.VMEM((HD, 2 * BLOCK), jnp.float32),
            ],
        ),
        compiler_params=pltpu.CompilerParams(vmem_limit_bytes=60 * 1024 * 1024),
        cost_estimate=pl.CostEstimate(
            flops=10 * 512 * 2560 * HD * HEADS,
            bytes_accessed=12000000,
            transcendentals=512 * 2560 * HEADS,
        ),
        name="attend",
    )(flags, bias, text_bias, qg, text, *blocks)
    return results[:2], results[2:5], results[5:7], results[7], results[8:]


def visibility(reach, ha, wa):
    between = lambda d, low, high: (d >= -low) & (d <= high)
    column = wa // 2 * 2
    s = jnp.arange(3, dtype=jnp.int32) - 1
    frames = between(s[None, :], reach[:, 0:1], reach[:, 1:2])
    frames = frames & (ha + s >= 0)[None, :] & (ha + s < FRAME_PARTS)[None, :]
    two = jnp.arange(2, dtype=jnp.int32)
    r = two[:, None] - two[None, :]
    rows = between(r[None], reach[:, 2, None, None], reach[:, 3, None, None])
    c = jnp.arange(4, dtype=jnp.int32) - 1
    d = c[:, None] - two[None, :]
    cols = between(d[None], reach[:, 4, None, None], reach[:, 5, None, None])
    cols = cols & ((column + c >= 0) & (column + c < COL_PARTS))[None, :, None]
    seen = (
        frames[:, :, None, None, None, None]
        & cols[:, None, :, None, :, None]
        & rows[:, None, None, :, None, :]
    )
    flags = jnp.any(seen, axis=(3, 4, 5)).astype(jnp.int32).reshape(HEADS * 12)
    bias = jnp.where(seen, 0.0, -jnp.inf).astype(jnp.float32).reshape(HEADS, 24, 4, 1)
    bias = jnp.broadcast_to(bias, (HEADS, 24, 4, 128)).reshape(HEADS, 24, 512)
    return flags, bias


def added(*parts):
    total = parts[0].astype(jnp.float32)
    for part in parts[1:]:
        total = total + part.astype(jnp.float32)
    return total.astype(jnp.bfloat16)


def halve_text(part, ha):
    upper = ha // RUN // 2
    other = lax.dynamic_slice_in_dim(part, (1 - upper) * (TEXT // 2), TEXT // 2, 0)
    return lax.dynamic_slice_in_dim(part, upper * (TEXT // 2), TEXT // 2, 0), move(other, flip(2 * RUN, 0))


def sum_text(part, group, ha, wa, beyond):
    upper, x = ha // RUN // 2, wa // 2
    pieces = [
        move(lax.dynamic_slice_in_dim(part, (x ^ d) * (TEXT // 8), TEXT // 8, 0), flip(0, 2 * d))
        for d in (1, 2, 3)
    ]
    part = added(lax.dynamic_slice_in_dim(part, x * (TEXT // 8), TEXT // 8, 0), *pieces)
    part, beyond[0], beyond[1] = lax.optimization_barrier((part, beyond[0], beyond[1]))
    near = [move(part, flip(d, 0)).astype(jnp.float32) for d in (1, 2, 3)]
    part = ((part.astype(jnp.float32) + near[0]) + (near[1] + near[2])).astype(jnp.bfloat16)
    mine = added(part, move(part, flip(RUN, 1)))
    theirs = added(move(part, flip(RUN, 0)), move(part, flip(0, 1)))
    both = jnp.stack(
        [jnp.where(group == 0, mine, theirs), jnp.where(group == 0, theirs, mine)], axis=0
    )
    quarter = jnp.zeros((4,) + both.shape, both.dtype)
    quarter = lax.dynamic_update_index_in_dim(quarter, both, x, 0)
    for d in (1, 2, 3):
        quarter = lax.dynamic_update_index_in_dim(quarter, move(both, flip(0, 2 * d)), x ^ d, 0)
    distant = move(quarter, flip(2 * RUN, 0))
    whole = jnp.stack(
        [jnp.where(upper == 0, quarter, distant), jnp.where(upper == 0, distant, quarter)], axis=0
    )
    whole = whole.reshape(2, 4, 2, TEXT // 8, HEADS, 2, HD)
    whole = whole.transpose(5, 0, 1, 3, 2, 4, 6).reshape(2, TEXT, 2 * HALF)
    whole = jnp.pad(whole, ((0, 0), (0, 256 - TEXT), (0, 0)))
    return whole[0], whole[1]


def body(
    queries, key_video, value_video, grad_output, text_keys, text_values, window_reach, text_valid
):
    ha, wa = lax.axis_index("ha"), lax.axis_index("wa")
    side = wa % 2
    group = (side + ha // RUN) % 2
    group_at = group.reshape(1).astype(jnp.int32)

    def placed(keep, got):
        return jnp.where(side == 0, keep, got), jnp.where(side == 0, got, keep)

    send_kv, keep_kv = split_heads(group_at, key_video, value_video)
    own = placed(keep_kv, move(send_kv, across))
    send_qg, keep_qg = split_heads(group_at, queries, grad_output)
    earlier = [move(block, frames_by(1)) for block in own]
    later = [move(block, frames_by(-1)) for block in own]
    beside = [move(own[1], cols_by(1)), move(own[0], cols_by(-1))]
    reach = lax.dynamic_slice_in_dim(window_reach, group * HEADS, HEADS, 0)
    flags, bias = visibility(reach, ha, wa)
    flags = jnp.concatenate([flags, side.reshape(1).astype(jnp.int32)])
    text_bias = jnp.where(text_valid[:TEXT] > 0, 0.0, -jnp.inf).astype(jnp.float32)
    text_bias = jnp.broadcast_to(text_bias[:, None], (TEXT, HD))
    text = jnp.stack(
        [
            lax.dynamic_slice_in_dim(t[:TEXT], group * HALF, HALF, 1).reshape(TEXT, HEADS, HD)
            for t in (text_keys, text_values)
        ],
        axis=2,
    ).reshape(TEXT, 2 * HALF)
    send_qg, keep_qg, flags, bias, text_bias, text, _, _, _ = lax.optimization_barrier(
        (send_qg, keep_qg, flags, bias, text_bias, text, earlier, later, beside)
    )
    qg = jnp.concatenate(placed(keep_qg, move(send_qg, across)), axis=0)

    blocks = []
    for left, right in (earlier, later):
        blocks += [move(right, cols_by(1)), left, right, move(left, cols_by(-1))]
    blocks[4:4] = [beside[0], *own, beside[1]]

    far, mids, (dq_own, dq_other), dtext, sides = attend(
        flags, bias, text_bias, qg, text, blocks
    )

    to_left = move(far[1], cols_by(1))
    to_right = move(far[0], cols_by(-1))
    dq_got = move(dq_other, across)
    dtext = halve_text(dtext, ha)
    to_left, to_right, dtext, sides = lax.optimization_barrier((to_left, to_right, dtext, sides))

    def frames(step):
        at = slice(step // 2 * BLOCK, (step // 2 + 1) * BLOCK)
        return added(mids[step], jnp.concatenate([to_left[at], to_right[at]], axis=0))

    outer = [move(frames(0), frames_by(-1)), move(frames(2), frames_by(1))]
    beyond = [move(sides[1], cols_by(1)), move(sides[0], cols_by(-1))]
    text_key_grad, text_value_grad = sum_text(added(*dtext), group, ha, wa, beyond)
    totals = added(mids[1], outer[0], outer[1], jnp.concatenate(beyond, axis=0))
    (query_grad,) = join_heads(group_at, dq_own, dq_got, join_one_kernel, 1)
    keep = jnp.where(side == 0, totals[:BLOCK], totals[BLOCK:])
    send = jnp.where(side == 0, totals[BLOCK:], totals[:BLOCK])
    key_grad, value_grad = join_heads(group_at, keep, move(send, across), join_pair_kernel, 2)
    return query_grad, key_grad, value_grad, text_key_grad, text_value_grad


def solution(mesh):
    video = P("ha", None, "wa", "ta")
    text = P(None, "ta")
    return jax.shard_map(
        body,
        mesh=mesh,
        in_specs=(video, video, video, video, text, text, P("ta", None), P()),
        out_specs=(video, video, video, text, text),
        check_vma=False,
    )
```

```python
import functools

import jax
import jax.numpy as jnp
import numpy as np
from jax import lax
from jax.experimental import pallas as pl
from jax.experimental.pallas import tpu as pltpu
from jax.sharding import PartitionSpec as P

HD = 128
TILE = 8
TILE_T = 2
AXES = ("ha", "wa")
FRAME_PARTS = 16
COL_PARTS = 8
RUN = 4
HEADS = 3
HALF = HEADS * HD
PAIR = 2 * HD
BLOCK = 256
TEXT = 192
SCALE = HD**-0.5
EXP_SCALE = SCALE * float(np.log2(np.e))
GROUPS = ((4,), (7,), (1, 2), (0,), (3,), (9, 10), (8,), (11,))
TILE_PARTS = ((0, 0, 0), (64, 1, 0), (128, 0, 1), (192, 1, 1))
COLS = ((0, 256), (0, 512), (0, 512), (256, 512))


def move(block, step):
    route = []
    for ha in range(FRAME_PARTS):
        for wa in range(COL_PARTS):
            there_ha, there_wa = step(ha, wa)
            if 0 <= there_ha < FRAME_PARTS and 0 <= there_wa < COL_PARTS:
                route.append((ha * COL_PARTS + wa, there_ha * COL_PARTS + there_wa))
    return lax.ppermute(block, AXES, route)


def across(ha, wa):
    return ha, wa ^ 1


def frames_by(distance):
    def step(ha, wa):
        there = ha + distance
        return there, wa ^ ((ha // RUN ^ there // RUN) & 1)

    return step


def cols_by(distance):
    return lambda ha, wa: (ha, wa + 2 * distance)


def flip(ha_bits, wa_bits):
    return lambda ha, wa: (ha ^ ha_bits, wa ^ wa_bits)


def lanes(start, count=HD):
    return pl.ds(pl.multiple_of(start, HD), count)


def split_kernel(group_ref, first_ref, second_ref, send_ref, keep_ref):
    group = group_ref[0]
    for out_ref, start in ((send_ref, (1 - group) * HALF), (keep_ref, group * HALF)):
        for at, frame, row in TILE_PARTS:
            for head in range(HEADS):
                for ref, low in ((first_ref, head * PAIR), (second_ref, head * PAIR + HD)):
                    part = ref[frame, row, :, lanes(start + head * HD)]
                    out_ref[at : at + 64, low : low + HD] = part


def split_heads(group, first, second):
    shape = (TILE_T, 2, TILE * TILE, 2 * HALF)
    source = pl.BlockSpec(shape, lambda i, g: (0, 0, 0, 0))
    target = pl.BlockSpec((BLOCK, 2 * HALF), lambda i, g: (0, 0))
    out = jax.ShapeDtypeStruct((BLOCK, 2 * HALF), jnp.bfloat16)
    return pl.pallas_call(
        split_kernel,
        out_shape=(out, out),
        grid_spec=pltpu.PrefetchScalarGridSpec(
            num_scalar_prefetch=1, grid=(1,), in_specs=[source, source], out_specs=(target, target)
        ),
        cost_estimate=pl.CostEstimate(flops=0, bytes_accessed=1600000, transcendentals=0),
        name="split_heads",
    )(group, first.reshape(shape), second.reshape(shape))


def join_pair_kernel(group_ref, keep_ref, got_ref, first_ref, second_ref):
    group = group_ref[0]
    for in_ref, start in ((keep_ref, group * HALF), (got_ref, (1 - group) * HALF)):
        for at, frame, row in TILE_PARTS:
            for head in range(HEADS):
                for ref, low in ((first_ref, head * PAIR), (second_ref, head * PAIR + HD)):
                    part = in_ref[at : at + 64, low : low + HD]
                    ref[frame, row, :, lanes(start + head * HD)] = part


def join_one_kernel(group_ref, keep_ref, got_ref, out_ref):
    group = group_ref[0]
    for in_ref, start in ((keep_ref, group * HALF), (got_ref, (1 - group) * HALF)):
        for at, frame, row in TILE_PARTS:
            out_ref[frame, row, :, lanes(start, HALF)] = in_ref[at : at + 64, :]


def join_heads(group, keep, got, kernel, count):
    shape = (TILE_T, 2, TILE * TILE, 2 * HALF)
    source = pl.BlockSpec(keep.shape, lambda i, g: (0, 0))
    target = pl.BlockSpec(shape, lambda i, g: (0, 0, 0, 0))
    out = jax.ShapeDtypeStruct(shape, jnp.bfloat16)
    parts = pl.pallas_call(
        kernel,
        out_shape=(out,) * count,
        grid_spec=pltpu.PrefetchScalarGridSpec(
            num_scalar_prefetch=1,
            grid=(1,),
            in_specs=[source, source],
            out_specs=(target,) * count,
        ),
        cost_estimate=pl.CostEstimate(flops=0, bytes_accessed=800000 * count, transcendentals=0),
        name="join_heads",
    )(group, keep, got)
    return [part.reshape(TILE_T, 2 * TILE, TILE, 2 * HALF) for part in parts]


def dot_t(left, right):
    return lax.dot_general(
        left, right, (((1,), (1,)), ((), ())), preferred_element_type=jnp.float32
    )


def dot(left, right):
    return lax.dot_general(
        left, right, (((1,), (0,)), ((), ())), preferred_element_type=jnp.float32
    )


def t_dot(left, right):
    return lax.dot_general(
        left, right, (((0,), (0,)), ((), ())), preferred_element_type=jnp.float32
    )


def fold(values, op):
    return op(values.reshape(values.shape[0] // 8, 8, values.shape[1]), axis=0)


def attend_kernel(flag_ref, bias_ref, text_bias_ref, keep_ref, got_ref, text_ref, *refs):
    kv_refs, far_refs, mid_refs = refs[:12], refs[12:14], refs[14:17]
    dq_refs, dtext_ref, side_refs = refs[17:19], refs[19], refs[20:22]
    qg_ref, p_ref, dp_ref, high_ref, total_ref, delta_ref, dq_sum_ref = refs[22:]
    head = pl.program_id(0)
    mirrored = flag_ref[36] != 0
    keep, got = keep_ref[...], got_ref[...]
    qg_ref[:BLOCK, :] = jnp.where(mirrored, got, keep)
    qg_ref[BLOCK:, :] = jnp.where(mirrored, keep, got)

    def visible(block):
        return flag_ref[head * 12 + block] != 0

    def q(low, high):
        return qg_ref[low:high, :HD]

    def g(low, high):
        return qg_ref[low:high, HD:]

    def rows(block):
        return slice(block * BLOCK, block * BLOCK + (TEXT if block == 12 else BLOCK))

    def grad(block):
        step, column = divmod(block, 4)
        if column in (1, 2):
            return mid_refs[step].at[rows(column - 1), :]
        if step == 1:
            return side_refs[column // 3]
        return far_refs[column // 3].at[rows(step // 2), :]

    def spare(block):
        return slice(block * 8, block * 8 + 8)

    def weigh(block, pair_ref, bias, low, high, start=False):
        width = high - low
        scores = dot_t(pair_ref[:, :HD], q(low, high))
        dp = dot_t(pair_ref[:, HD:], g(low, high))
        dp_ref[rows(block), low:high] = dp
        if start:
            scores = scores + bias
        else:
            scores = (scores.reshape(2, 128, width) + bias[:, None, :]).reshape(BLOCK, width)
        highest = fold(scores, jnp.max)
        if not start:
            old = high_ref[spare(12), low:high]
            highest = jnp.maximum(old, highest)
            shrink = jnp.exp2((old - highest) * EXP_SCALE)
        p = jnp.exp2((scores.reshape(-1, 8, width) - highest[None]) * EXP_SCALE)
        total, delta = jnp.sum(p, axis=0), jnp.sum(p * dp.reshape(-1, 8, width), axis=0)
        p_ref[rows(block), low:high] = p.reshape(-1, width)
        if not start:
            total = total + total_ref[:, low:high] * shrink
            delta = delta + delta_ref[:, low:high] * shrink
            high_ref[spare(block), low:high] = highest
        else:
            high_ref[spare(13), low:high] = highest
        high_ref[spare(12), low:high] = highest
        total_ref[:, low:high] = total
        delta_ref[:, low:high] = delta

    weigh(12, text_ref, text_bias_ref[:, :1], 0, 512, start=True)
    def weigh_all(group):
        for block in group:
            low, high = COLS[block % 4]
            bias = bias_ref[0, 2 * block : 2 * block + 2, low:high]
            weigh(block, kv_refs[block], bias, low, high)

    weigh_all((5, 6))
    for group in GROUPS:
        pl.when(visible(group[0]))(functools.partial(weigh_all, group))

    last = high_ref[spare(12), :]
    highest = jnp.max(last, axis=0, keepdims=True)
    shrink = jnp.exp2((last - highest) * EXP_SCALE)
    inverse = 1.0 / jnp.sum(total_ref[...] * shrink, axis=0, keepdims=True)
    delta = jnp.sum(delta_ref[...] * shrink, axis=0, keepdims=True) * inverse

    def spread(block, key, out_ref, low, high):
        width = high - low
        at = spare(block + (block == 12))
        shrink = jnp.exp2((high_ref[at, low:high] - highest[:, low:high]) * EXP_SCALE)
        shrink = shrink * inverse[:, low:high]
        prob = p_ref[rows(block), low:high].reshape(-1, 8, width) * shrink[None]
        prob = prob.reshape(-1, width)
        ds = prob * ((dp_ref[rows(block), low:high] - delta[:, low:high]) * SCALE)
        ds = ds.astype(jnp.bfloat16)
        prob = prob.astype(jnp.bfloat16)
        out_ref[:, :HD] = dot(ds, q(low, high)).astype(jnp.bfloat16)
        out_ref[:, HD:] = dot(prob, g(low, high)).astype(jnp.bfloat16)
        return t_dot(key, ds)

    dq_sum_ref[...] = spread(12, text_ref[:, :HD], dtext_ref, 0, 512)
    def spread_all(group):
        for block in group:
            low, high = COLS[block % 4]
            dq_sum_ref[:, low:high] += spread(
                block, kv_refs[block][:, :HD], grad(block), low, high
            )

    def clear_all(group):
        for block in group:
            grad(block)[...] = jnp.zeros((BLOCK, PAIR), jnp.bfloat16)

    spread_all((5, 6))
    for group in GROUPS:
        pl.when(visible(group[0]))(functools.partial(spread_all, group))
        pl.when(jnp.logical_not(visible(group[0])))(functools.partial(clear_all, group))

    for ref, low, high in zip(dq_refs, (0, BLOCK), (BLOCK, 0)):
        sums = jnp.where(
            mirrored, dq_sum_ref[:, high : high + BLOCK], dq_sum_ref[:, low : low + BLOCK]
        )
        ref[...] = sums.T.astype(jnp.bfloat16)


def attend(flags, bias, text_bias, keep_qg, got_qg, text, blocks):
    pair = pl.BlockSpec((BLOCK, PAIR), lambda h, f: (0, h))
    text_pair = pl.BlockSpec((TEXT, PAIR), lambda h, f: (0, h))
    text_out = jax.ShapeDtypeStruct((TEXT, 2 * HALF), jnp.bfloat16)
    wide = pl.BlockSpec((2 * BLOCK, PAIR), lambda h, f: (0, h))
    out = jax.ShapeDtypeStruct((BLOCK, 2 * HALF), jnp.bfloat16)
    wide_out = jax.ShapeDtypeStruct((2 * BLOCK, 2 * HALF), jnp.bfloat16)
    results = pl.pallas_call(
        attend_kernel,
        out_shape=(wide_out,) * 2
        + (wide_out,) * 3
        + (jax.ShapeDtypeStruct((BLOCK, HALF), jnp.bfloat16),) * 2
        + (text_out,)
        + (out,) * 2,
        grid_spec=pltpu.PrefetchScalarGridSpec(
            num_scalar_prefetch=1,
            grid=(HEADS,),
            in_specs=[
                pl.BlockSpec((1, 24, 2 * BLOCK), lambda h, f: (h, 0, 0)),
                pl.BlockSpec((TEXT, HD), lambda h, f: (0, 0)),
                pair,
                pair,
                text_pair,
            ]
            + [pair] * 12,
            out_specs=(wide,) * 2
            + (wide,) * 3
            + (pl.BlockSpec((BLOCK, HD), lambda h, f: (0, h)),) * 2
            + (text_pair,)
            + (pair,) * 2,
            scratch_shapes=[
                pltpu.VMEM((2 * BLOCK, PAIR), jnp.bfloat16),
                pltpu.VMEM((13 * BLOCK, 2 * BLOCK), jnp.float32),
                pltpu.VMEM((13 * BLOCK, 2 * BLOCK), jnp.float32),
                pltpu.VMEM((8 * 14, 2 * BLOCK), jnp.float32),
                pltpu.VMEM((8, 2 * BLOCK), jnp.float32),
                pltpu.VMEM((8, 2 * BLOCK), jnp.float32),
                pltpu.VMEM((HD, 2 * BLOCK), jnp.float32),
            ],
        ),
        compiler_params=pltpu.CompilerParams(vmem_limit_bytes=60 * 1024 * 1024),
        cost_estimate=pl.CostEstimate(
            flops=10 * 512 * 2560 * HD * HEADS,
            bytes_accessed=12000000,
            transcendentals=512 * 2560 * HEADS,
        ),
        name="attend",
    )(flags, bias, text_bias, keep_qg, got_qg, text, *blocks)
    return results[:2], results[2:5], results[5:7], results[7], results[8:]


def visibility(reach, ha, wa):
    between = lambda d, low, high: (d >= -low) & (d <= high)
    column = wa // 2 * 2
    s = jnp.arange(3, dtype=jnp.int32) - 1
    frames = between(s[None, :], reach[:, 0:1], reach[:, 1:2])
    frames = frames & (ha + s >= 0)[None, :] & (ha + s < FRAME_PARTS)[None, :]
    two = jnp.arange(2, dtype=jnp.int32)
    r = two[:, None] - two[None, :]
    rows = between(r[None], reach[:, 2, None, None], reach[:, 3, None, None])
    c = jnp.arange(4, dtype=jnp.int32) - 1
    d = c[:, None] - two[None, :]
    cols = between(d[None], reach[:, 4, None, None], reach[:, 5, None, None])
    cols = cols & ((column + c >= 0) & (column + c < COL_PARTS))[None, :, None]
    seen = (
        frames[:, :, None, None, None, None]
        & cols[:, None, :, None, :, None]
        & rows[:, None, None, :, None, :]
    )
    flags = jnp.any(seen, axis=(3, 4, 5)).astype(jnp.int32).reshape(HEADS * 12)
    bias = jnp.where(seen, 0.0, -jnp.inf).astype(jnp.float32).reshape(HEADS, 24, 4, 1)
    bias = jnp.broadcast_to(bias, (HEADS, 24, 4, 128)).reshape(HEADS, 24, 512)
    return flags, bias


def added(*parts):
    total = parts[0].astype(jnp.float32)
    for part in parts[1:]:
        total = total + part.astype(jnp.float32)
    return total.astype(jnp.bfloat16)


def halve_text(part, ha):
    upper = ha // RUN // 2
    other = lax.dynamic_slice_in_dim(part, (1 - upper) * (TEXT // 2), TEXT // 2, 0)
    mine = lax.dynamic_slice_in_dim(part, upper * (TEXT // 2), TEXT // 2, 0)
    return mine, move(other, flip(2 * RUN, 0))


def sum_text(part, group, ha, wa, beyond):
    upper, x = ha // RUN // 2, wa // 2
    pieces = [
        move(lax.dynamic_slice_in_dim(part, (x ^ d) * (TEXT // 8), TEXT // 8, 0), flip(0, 2 * d))
        for d in (1, 2, 3)
    ]
    part = added(lax.dynamic_slice_in_dim(part, x * (TEXT // 8), TEXT // 8, 0), *pieces)
    near = [move(part, flip(d, 0)).astype(jnp.float32) for d in (1, 2, 3)]
    part = ((part.astype(jnp.float32) + near[0]) + (near[1] + near[2])).astype(jnp.bfloat16)
    mine = added(part, move(part, flip(RUN, 1)))
    theirs = added(move(part, flip(RUN, 0)), move(part, flip(0, 1)))
    both = jnp.stack(
        [jnp.where(group == 0, mine, theirs), jnp.where(group == 0, theirs, mine)], axis=0
    )
    both, beyond[0], beyond[1] = lax.optimization_barrier((both, beyond[0], beyond[1]))
    quarter = jnp.zeros((4,) + both.shape, both.dtype)
    quarter = lax.dynamic_update_index_in_dim(quarter, both, x, 0)
    for d in (1, 2, 3):
        quarter = lax.dynamic_update_index_in_dim(quarter, move(both, flip(0, 2 * d)), x ^ d, 0)
    distant = move(quarter, flip(2 * RUN, 0))
    whole = jnp.stack(
        [jnp.where(upper == 0, quarter, distant), jnp.where(upper == 0, distant, quarter)], axis=0
    )
    whole = whole.reshape(2, 4, 2, TEXT // 8, HEADS, 2, HD)
    whole = whole.transpose(5, 0, 1, 3, 2, 4, 6).reshape(2, TEXT, 2 * HALF)
    whole = jnp.pad(whole, ((0, 0), (0, 256 - TEXT), (0, 0)))
    return whole[0], whole[1]


def body(
    queries, key_video, value_video, grad_output, text_keys, text_values, window_reach, text_valid
):
    ha, wa = lax.axis_index("ha"), lax.axis_index("wa")
    side = wa % 2
    group = (side + ha // RUN) % 2
    group_at = group.reshape(1).astype(jnp.int32)

    def placed(keep, got):
        return jnp.where(side == 0, keep, got), jnp.where(side == 0, got, keep)

    send_kv, keep_kv = split_heads(group_at, key_video, value_video)
    own = placed(keep_kv, move(send_kv, across))
    send_qg, keep_qg = split_heads(group_at, queries, grad_output)
    earlier = [move(block, frames_by(1)) for block in own]
    later = [move(block, frames_by(-1)) for block in own]
    beside = [move(own[1], cols_by(1)), move(own[0], cols_by(-1))]
    reach = lax.dynamic_slice_in_dim(window_reach, group * HEADS, HEADS, 0)
    flags, bias = visibility(reach, ha, wa)
    flags = jnp.concatenate([flags, side.reshape(1).astype(jnp.int32)])
    text_bias = jnp.where(text_valid[:TEXT] > 0, 0.0, -jnp.inf).astype(jnp.float32)
    text_bias = jnp.broadcast_to(text_bias[:, None], (TEXT, HD))
    text = jnp.stack(
        [
            lax.dynamic_slice_in_dim(t[:TEXT], group * HALF, HALF, 1).reshape(TEXT, HEADS, HD)
            for t in (text_keys, text_values)
        ],
        axis=2,
    ).reshape(TEXT, 2 * HALF)
    send_qg, keep_qg, flags, bias, text_bias, text, _, _ = lax.optimization_barrier(
        (send_qg, keep_qg, flags, bias, text_bias, text, earlier[0], later[0])
    )
    got_qg = move(send_qg, across)

    blocks = []
    for left, right in (earlier, later):
        blocks += [move(right, cols_by(1)), left, right, move(left, cols_by(-1))]
    blocks[4:4] = [beside[0], *own, beside[1]]

    far, mids, (dq_own, dq_other), dtext, sides = attend(
        flags, bias, text_bias, keep_qg, got_qg, text, blocks
    )

    to_left = move(far[1], cols_by(1))
    to_right = move(far[0], cols_by(-1))
    dq_got = move(dq_other, across)
    dtext = halve_text(dtext, ha)
    to_left, to_right, dtext, sides = lax.optimization_barrier((to_left, to_right, dtext, sides))

    def frames(step):
        at = slice(step // 2 * BLOCK, (step // 2 + 1) * BLOCK)
        return added(mids[step], jnp.concatenate([to_left[at], to_right[at]], axis=0))

    outer = [move(frames(0), frames_by(-1)), move(frames(2), frames_by(1))]
    beyond = [move(sides[1], cols_by(1)), move(sides[0], cols_by(-1))]
    text_key_grad, text_value_grad = sum_text(added(*dtext), group, ha, wa, beyond)
    totals = added(mids[1], outer[0], outer[1], jnp.concatenate(beyond, axis=0))
    (query_grad,) = join_heads(group_at, dq_own, dq_got, join_one_kernel, 1)
    keep = jnp.where(side == 0, totals[:BLOCK], totals[BLOCK:])
    send = jnp.where(side == 0, totals[BLOCK:], totals[:BLOCK])
    key_grad, value_grad = join_heads(group_at, keep, move(send, across), join_pair_kernel, 2)
    return query_grad, key_grad, value_grad, text_key_grad, text_value_grad


def solution(mesh):
    video = P("ha", None, "wa", "ta")
    text = P(None, "ta")
    return jax.shard_map(
        body,
        mesh=mesh,
        in_specs=(video, video, video, video, text, text, P("ta", None), P()),
        out_specs=(video, video, video, text, text),
        check_vma=False,
    )
```

```python
import functools

import jax
import jax.numpy as jnp
import numpy as np
from jax import lax
from jax.experimental import pallas as pl
from jax.experimental.pallas import tpu as pltpu
from jax.sharding import PartitionSpec as P

HD = 128
TILE = 8
TILE_T = 2
AXES = ("ha", "wa")
FRAME_PARTS = 16
COL_PARTS = 8
RUN = 4
HEADS = 3
HALF = HEADS * HD
PAIR = 2 * HD
BLOCK = 256
TEXT = 192
SCALE = HD**-0.5
EXP_SCALE = SCALE * float(np.log2(np.e))
GROUPS = ((4,), (7,), (1, 2), (0,), (3,), (9, 10), (8,), (11,))
TILE_PARTS = ((0, 0, 0), (64, 1, 0), (128, 0, 1), (192, 1, 1))
COLS = ((0, 256), (0, 512), (0, 512), (256, 512))


def move(block, step):
    route = []
    for ha in range(FRAME_PARTS):
        for wa in range(COL_PARTS):
            there_ha, there_wa = step(ha, wa)
            if 0 <= there_ha < FRAME_PARTS and 0 <= there_wa < COL_PARTS:
                route.append((ha * COL_PARTS + wa, there_ha * COL_PARTS + there_wa))
    return lax.ppermute(block, AXES, route)


def across(ha, wa):
    return ha, wa ^ 1


def frames_by(distance):
    def step(ha, wa):
        there = ha + distance
        return there, wa ^ ((ha // RUN ^ there // RUN) & 1)

    return step


def cols_by(distance):
    return lambda ha, wa: (ha, wa + 2 * distance)


def flip(ha_bits, wa_bits):
    return lambda ha, wa: (ha ^ ha_bits, wa ^ wa_bits)


def lanes(start, count=HD):
    return pl.ds(pl.multiple_of(start, HD), count)


def split_kernel(group_ref, first_ref, second_ref, send_ref, keep_ref):
    group = group_ref[0]
    for out_ref, start in ((send_ref, (1 - group) * HALF), (keep_ref, group * HALF)):
        for at, frame, row in TILE_PARTS:
            for head in range(HEADS):
                for ref, low in ((first_ref, head * PAIR), (second_ref, head * PAIR + HD)):
                    part = ref[frame, row, :, lanes(start + head * HD)]
                    out_ref[at : at + 64, low : low + HD] = part


def split_heads(group, first, second):
    shape = (TILE_T, 2, TILE * TILE, 2 * HALF)
    source = pl.BlockSpec(shape, lambda i, g: (0, 0, 0, 0))
    target = pl.BlockSpec((BLOCK, 2 * HALF), lambda i, g: (0, 0))
    out = jax.ShapeDtypeStruct((BLOCK, 2 * HALF), jnp.bfloat16)
    return pl.pallas_call(
        split_kernel,
        out_shape=(out, out),
        grid_spec=pltpu.PrefetchScalarGridSpec(
            num_scalar_prefetch=1, grid=(1,), in_specs=[source, source], out_specs=(target, target)
        ),
        cost_estimate=pl.CostEstimate(flops=0, bytes_accessed=1600000, transcendentals=0),
        name="split_heads",
    )(group, first.reshape(shape), second.reshape(shape))


def join_pair_kernel(group_ref, keep_ref, got_ref, first_ref, second_ref):
    group = group_ref[0]
    for in_ref, start in ((keep_ref, group * HALF), (got_ref, (1 - group) * HALF)):
        for at, frame, row in TILE_PARTS:
            for head in range(HEADS):
                for ref, low in ((first_ref, head * PAIR), (second_ref, head * PAIR + HD)):
                    part = in_ref[at : at + 64, low : low + HD]
                    ref[frame, row, :, lanes(start + head * HD)] = part


def join_one_kernel(group_ref, keep_ref, got_ref, out_ref):
    group = group_ref[0]
    for in_ref, start in ((keep_ref, group * HALF), (got_ref, (1 - group) * HALF)):
        for at, frame, row in TILE_PARTS:
            out_ref[frame, row, :, lanes(start, HALF)] = in_ref[at : at + 64, :]


def join_heads(group, keep, got, kernel, count):
    shape = (TILE_T, 2, TILE * TILE, 2 * HALF)
    source = pl.BlockSpec(keep.shape, lambda i, g: (0, 0))
    target = pl.BlockSpec(shape, lambda i, g: (0, 0, 0, 0))
    out = jax.ShapeDtypeStruct(shape, jnp.bfloat16)
    parts = pl.pallas_call(
        kernel,
        out_shape=(out,) * count,
        grid_spec=pltpu.PrefetchScalarGridSpec(
            num_scalar_prefetch=1,
            grid=(1,),
            in_specs=[source, source],
            out_specs=(target,) * count,
        ),
        cost_estimate=pl.CostEstimate(flops=0, bytes_accessed=800000 * count, transcendentals=0),
        name="join_heads",
    )(group, keep, got)
    return [part.reshape(TILE_T, 2 * TILE, TILE, 2 * HALF) for part in parts]


def dot_t(left, right):
    return lax.dot_general(
        left, right, (((1,), (1,)), ((), ())), preferred_element_type=jnp.float32
    )


def dot(left, right):
    return lax.dot_general(
        left, right, (((1,), (0,)), ((), ())), preferred_element_type=jnp.float32
    )


def t_dot(left, right):
    return lax.dot_general(
        left, right, (((0,), (0,)), ((), ())), preferred_element_type=jnp.float32
    )


def fold(values, op):
    return op(values.reshape(values.shape[0] // 8, 8, values.shape[1]), axis=0)


def attend_kernel(flag_ref, bias_ref, text_bias_ref, keep_ref, got_ref, text_ref, *refs):
    kv_refs, far_refs, mid_refs = refs[:12], refs[12:14], refs[14:17]
    dq_refs, dtext_ref, side_refs = refs[17:19], refs[19], refs[20:22]
    qg_ref, p_ref, dp_ref, high_ref, total_ref, delta_ref, dq_sum_ref = refs[22:]
    head = pl.program_id(0)
    mirrored = flag_ref[36] != 0
    keep, got = keep_ref[...], got_ref[...]
    qg_ref[:BLOCK, :] = jnp.where(mirrored, got, keep)
    qg_ref[BLOCK:, :] = jnp.where(mirrored, keep, got)

    def visible(block):
        return flag_ref[head * 12 + block] != 0

    def q(low, high):
        return qg_ref[low:high, :HD]

    def g(low, high):
        return qg_ref[low:high, HD:]

    def rows(block):
        return slice(block * BLOCK, block * BLOCK + (TEXT if block == 12 else BLOCK))

    def grad(block):
        step, column = divmod(block, 4)
        if column in (1, 2):
            return mid_refs[step].at[rows(column - 1), :]
        if step == 1:
            return side_refs[column // 3]
        return far_refs[column // 3].at[rows(step // 2), :]

    def spare(block):
        return slice(block * 8, block * 8 + 8)

    def weigh(block, pair_ref, bias, low, high, start=False):
        width = high - low
        scores = dot_t(pair_ref[:, :HD], q(low, high))
        dp = dot_t(pair_ref[:, HD:], g(low, high))
        dp_ref[rows(block), low:high] = dp
        if start:
            scores = scores + bias
        else:
            scores = (scores.reshape(2, 128, width) + bias[:, None, :]).reshape(BLOCK, width)
        highest = fold(scores, jnp.max)
        if not start:
            old = high_ref[spare(12), low:high]
            highest = jnp.maximum(old, highest)
            shrink = jnp.exp2((old - highest) * EXP_SCALE)
        p = jnp.exp2((scores.reshape(-1, 8, width) - highest[None]) * EXP_SCALE)
        total, delta = jnp.sum(p, axis=0), jnp.sum(p * dp.reshape(-1, 8, width), axis=0)
        p_ref[rows(block), low:high] = p.reshape(-1, width)
        if not start:
            total = total + total_ref[:, low:high] * shrink
            delta = delta + delta_ref[:, low:high] * shrink
            high_ref[spare(block), low:high] = highest
        else:
            high_ref[spare(13), low:high] = highest
        high_ref[spare(12), low:high] = highest
        total_ref[:, low:high] = total
        delta_ref[:, low:high] = delta

    weigh(12, text_ref, text_bias_ref[:, :1], 0, 512, start=True)
    def weigh_all(group):
        for block in group:
            low, high = COLS[block % 4]
            bias = bias_ref[0, 2 * block : 2 * block + 2, low:high]
            weigh(block, kv_refs[block], bias, low, high)

    weigh_all((5, 6))
    for group in GROUPS:
        pl.when(visible(group[0]))(functools.partial(weigh_all, group))

    last = high_ref[spare(12), :]
    highest = jnp.max(last, axis=0, keepdims=True)
    shrink = jnp.exp2((last - highest) * EXP_SCALE)
    inverse = 1.0 / jnp.sum(total_ref[...] * shrink, axis=0, keepdims=True)
    delta = jnp.sum(delta_ref[...] * shrink, axis=0, keepdims=True) * inverse

    def spread(block, key, out_ref, low, high):
        width = high - low
        at = spare(block + (block == 12))
        shrink = jnp.exp2((high_ref[at, low:high] - highest[:, low:high]) * EXP_SCALE)
        shrink = shrink * inverse[:, low:high]
        prob = p_ref[rows(block), low:high].reshape(-1, 8, width) * shrink[None]
        prob = prob.reshape(-1, width)
        ds = prob * ((dp_ref[rows(block), low:high] - delta[:, low:high]) * SCALE)
        ds = ds.astype(jnp.bfloat16)
        prob = prob.astype(jnp.bfloat16)
        out_ref[:, :HD] = dot(ds, q(low, high)).astype(jnp.bfloat16)
        out_ref[:, HD:] = dot(prob, g(low, high)).astype(jnp.bfloat16)
        return t_dot(key, ds)

    dq_sum_ref[...] = spread(12, text_ref[:, :HD], dtext_ref, 0, 512)
    def spread_all(group):
        for block in group:
            low, high = COLS[block % 4]
            dq_sum_ref[:, low:high] += spread(
                block, kv_refs[block][:, :HD], grad(block), low, high
            )

    def clear_all(group):
        for block in group:
            grad(block)[...] = jnp.zeros((BLOCK, PAIR), jnp.bfloat16)

    spread_all((5, 6))
    for group in GROUPS:
        pl.when(visible(group[0]))(functools.partial(spread_all, group))
        pl.when(jnp.logical_not(visible(group[0])))(functools.partial(clear_all, group))

    for ref, low, high in zip(dq_refs, (0, BLOCK), (BLOCK, 0)):
        sums = jnp.where(
            mirrored, dq_sum_ref[:, high : high + BLOCK], dq_sum_ref[:, low : low + BLOCK]
        )
        ref[...] = sums.T.astype(jnp.bfloat16)


def attend(flags, bias, text_bias, keep_qg, got_qg, text, blocks):
    pair = pl.BlockSpec((BLOCK, PAIR), lambda h, f: (0, h))
    text_pair = pl.BlockSpec((TEXT, PAIR), lambda h, f: (0, h))
    text_out = jax.ShapeDtypeStruct((TEXT, 2 * HALF), jnp.bfloat16)
    wide = pl.BlockSpec((2 * BLOCK, PAIR), lambda h, f: (0, h))
    out = jax.ShapeDtypeStruct((BLOCK, 2 * HALF), jnp.bfloat16)
    wide_out = jax.ShapeDtypeStruct((2 * BLOCK, 2 * HALF), jnp.bfloat16)
    results = pl.pallas_call(
        attend_kernel,
        out_shape=(wide_out,) * 2
        + (wide_out,) * 3
        + (jax.ShapeDtypeStruct((BLOCK, HALF), jnp.bfloat16),) * 2
        + (text_out,)
        + (out,) * 2,
        grid_spec=pltpu.PrefetchScalarGridSpec(
            num_scalar_prefetch=1,
            grid=(HEADS,),
            in_specs=[
                pl.BlockSpec((1, 24, 2 * BLOCK), lambda h, f: (h, 0, 0)),
                pl.BlockSpec((TEXT, HD), lambda h, f: (0, 0)),
                pair,
                pair,
                text_pair,
            ]
            + [pair] * 12,
            out_specs=(wide,) * 2
            + (wide,) * 3
            + (pl.BlockSpec((BLOCK, HD), lambda h, f: (0, h)),) * 2
            + (text_pair,)
            + (pair,) * 2,
            scratch_shapes=[
                pltpu.VMEM((2 * BLOCK, PAIR), jnp.bfloat16),
                pltpu.VMEM((13 * BLOCK, 2 * BLOCK), jnp.float32),
                pltpu.VMEM((13 * BLOCK, 2 * BLOCK), jnp.float32),
                pltpu.VMEM((8 * 14, 2 * BLOCK), jnp.float32),
                pltpu.VMEM((8, 2 * BLOCK), jnp.float32),
                pltpu.VMEM((8, 2 * BLOCK), jnp.float32),
                pltpu.VMEM((HD, 2 * BLOCK), jnp.float32),
            ],
        ),
        compiler_params=pltpu.CompilerParams(vmem_limit_bytes=60 * 1024 * 1024),
        cost_estimate=pl.CostEstimate(
            flops=10 * 512 * 2560 * HD * HEADS,
            bytes_accessed=12000000,
            transcendentals=512 * 2560 * HEADS,
        ),
        name="attend",
    )(flags, bias, text_bias, keep_qg, got_qg, text, *blocks)
    return results[:2], results[2:5], results[5:7], results[7], results[8:]


def visibility(reach, ha, wa):
    between = lambda d, low, high: (d >= -low) & (d <= high)
    column = wa // 2 * 2
    s = jnp.arange(3, dtype=jnp.int32) - 1
    frames = between(s[None, :], reach[:, 0:1], reach[:, 1:2])
    frames = frames & (ha + s >= 0)[None, :] & (ha + s < FRAME_PARTS)[None, :]
    two = jnp.arange(2, dtype=jnp.int32)
    r = two[:, None] - two[None, :]
    rows = between(r[None], reach[:, 2, None, None], reach[:, 3, None, None])
    c = jnp.arange(4, dtype=jnp.int32) - 1
    d = c[:, None] - two[None, :]
    cols = between(d[None], reach[:, 4, None, None], reach[:, 5, None, None])
    cols = cols & ((column + c >= 0) & (column + c < COL_PARTS))[None, :, None]
    seen = (
        frames[:, :, None, None, None, None]
        & cols[:, None, :, None, :, None]
        & rows[:, None, None, :, None, :]
    )
    flags = jnp.any(seen, axis=(3, 4, 5)).astype(jnp.int32).reshape(HEADS * 12)
    bias = jnp.where(seen, 0.0, -jnp.inf).astype(jnp.float32).reshape(HEADS, 24, 4, 1)
    bias = jnp.broadcast_to(bias, (HEADS, 24, 4, 128)).reshape(HEADS, 24, 512)
    return flags, bias


def added(*parts):
    total = parts[0].astype(jnp.float32)
    for part in parts[1:]:
        total = total + part.astype(jnp.float32)
    return total.astype(jnp.bfloat16)


def halve_text(part, ha):
    upper = ha // RUN // 2
    other = lax.dynamic_slice_in_dim(part, (1 - upper) * (TEXT // 2), TEXT // 2, 0)
    mine = lax.dynamic_slice_in_dim(part, upper * (TEXT // 2), TEXT // 2, 0)
    return mine, move(other, flip(2 * RUN, 0))


def sum_text(part, group, ha, wa, beyond):
    upper, x = ha // RUN // 2, wa // 2
    pieces = [
        move(lax.dynamic_slice_in_dim(part, (x ^ d) * (TEXT // 8), TEXT // 8, 0), flip(0, 2 * d))
        for d in (1, 2, 3)
    ]
    part = added(lax.dynamic_slice_in_dim(part, x * (TEXT // 8), TEXT // 8, 0), *pieces)
    near = [move(part, flip(d, 0)).astype(jnp.float32) for d in (1, 2, 3)]
    part = ((part.astype(jnp.float32) + near[0]) + (near[1] + near[2])).astype(jnp.bfloat16)
    mine = added(part, move(part, flip(RUN, 1)))
    theirs = added(move(part, flip(RUN, 0)), move(part, flip(0, 1)))
    both = jnp.stack(
        [jnp.where(group == 0, mine, theirs), jnp.where(group == 0, theirs, mine)], axis=0
    )
    both, beyond[0], beyond[1] = lax.optimization_barrier((both, beyond[0], beyond[1]))
    quarter = jnp.zeros((4,) + both.shape, both.dtype)
    quarter = lax.dynamic_update_index_in_dim(quarter, both, x, 0)
    for d in (1, 2, 3):
        quarter = lax.dynamic_update_index_in_dim(quarter, move(both, flip(0, 2 * d)), x ^ d, 0)
    distant = move(quarter, flip(2 * RUN, 0))
    whole = jnp.stack(
        [jnp.where(upper == 0, quarter, distant), jnp.where(upper == 0, distant, quarter)], axis=0
    )
    whole = whole.reshape(2, 4, 2, TEXT // 8, HEADS, 2, HD)
    whole = whole.transpose(5, 0, 1, 3, 2, 4, 6).reshape(2, TEXT, 2 * HALF)
    whole = jnp.pad(whole, ((0, 0), (0, 256 - TEXT), (0, 0)))
    return whole[0], whole[1]


def body(
    queries, key_video, value_video, grad_output, text_keys, text_values, window_reach, text_valid
):
    ha, wa = lax.axis_index("ha"), lax.axis_index("wa")
    side = wa % 2
    group = (side + ha // RUN) % 2
    group_at = group.reshape(1).astype(jnp.int32)

    def placed(keep, got):
        return jnp.where(side == 0, keep, got), jnp.where(side == 0, got, keep)

    send_kv, keep_kv = split_heads(group_at, key_video, value_video)
    own = placed(keep_kv, move(send_kv, across))
    send_qg, keep_qg = split_heads(group_at, queries, grad_output)
    earlier = [move(block, frames_by(1)) for block in own]
    later = [move(block, frames_by(-1)) for block in own]
    beside = [move(own[1], cols_by(1)), move(own[0], cols_by(-1))]
    reach = lax.dynamic_slice_in_dim(window_reach, group * HEADS, HEADS, 0)
    flags, bias = visibility(reach, ha, wa)
    flags = jnp.concatenate([flags, side.reshape(1).astype(jnp.int32)])
    text_bias = jnp.where(text_valid[:TEXT] > 0, 0.0, -jnp.inf).astype(jnp.float32)
    text_bias = jnp.broadcast_to(text_bias[:, None], (TEXT, HD))
    text = jnp.stack(
        [
            lax.dynamic_slice_in_dim(t[:TEXT], group * HALF, HALF, 1).reshape(TEXT, HEADS, HD)
            for t in (text_keys, text_values)
        ],
        axis=2,
    ).reshape(TEXT, 2 * HALF)
    send_qg, keep_qg, flags, bias, text_bias, text, _, _ = lax.optimization_barrier(
        (send_qg, keep_qg, flags, bias, text_bias, text, earlier[0], later[0])
    )
    got_qg = move(send_qg, across)

    blocks = []
    for left, right in (earlier, later):
        blocks += [move(right, cols_by(1)), left, right, move(left, cols_by(-1))]
    blocks[4:4] = [beside[0], *own, beside[1]]

    far, mids, (dq_own, dq_other), dtext, sides = attend(
        flags, bias, text_bias, keep_qg, got_qg, text, blocks
    )

    to_left = move(far[1], cols_by(1))
    to_right = move(far[0], cols_by(-1))
    dq_got = move(dq_other, across)
    dtext = halve_text(dtext, ha)
    to_left, to_right, dtext, sides = lax.optimization_barrier((to_left, to_right, dtext, sides))

    def frames(step):
        at = slice(step // 2 * BLOCK, (step // 2 + 1) * BLOCK)
        return added(mids[step], jnp.concatenate([to_left[at], to_right[at]], axis=0))

    outer = [move(frames(0), frames_by(-1)), move(frames(2), frames_by(1))]
    beyond = [move(sides[1], cols_by(1)), move(sides[0], cols_by(-1))]
    text_key_grad, text_value_grad = sum_text(added(*dtext), group, ha, wa, beyond)
    totals = added(mids[1], outer[0], outer[1], jnp.concatenate(beyond, axis=0))
    totals, dq_own, dq_got = lax.optimization_barrier((totals, dq_own, dq_got))
    (query_grad,) = join_heads(group_at, dq_own, dq_got, join_one_kernel, 1)
    keep = jnp.where(side == 0, totals[:BLOCK], totals[BLOCK:])
    send = jnp.where(side == 0, totals[BLOCK:], totals[:BLOCK])
    key_grad, value_grad = join_heads(group_at, keep, move(send, across), join_pair_kernel, 2)
    return query_grad, key_grad, value_grad, text_key_grad, text_value_grad


def solution(mesh):
    video = P("ha", None, "wa", "ta")
    text = P(None, "ta")
    return jax.shard_map(
        body,
        mesh=mesh,
        in_specs=(video, video, video, video, text, text, P("ta", None), P()),
        out_specs=(video, video, video, text, text),
        check_vma=False,
    )
```
